512 devices in a mesh: cp: 64 (over z, y), hd: 8 (over x, core).
Axes of the slice: x: 4, y: 4, z: 16, core: 2. Of those that a mesh axis runs over, the one named last changes fastest.
Arguments:
- queries: bfloat16 [32768, 4096], P(('cp', 'hd')), may hold values from -10 to 10
- keys: bfloat16 [32768, 1024], P(('cp', 'hd')), may hold values from -10 to 10
- values: bfloat16 [32768, 1024], P(('cp', 'hd')), may hold values from -6 to 6
- doc_starts: int32 [16], replicated, may hold values from 0 to 28672, as said below
Outputs:
- attended: bfloat16 [32768, 4096], P(('cp', 'hd'))
The draws below stay inside these ranges and needn't reach their ends.
Inputs may be any that keep to these rules, and one draw needn't show every extreme that they name: `doc_starts`: offsets rise strictly from 0; every document holds 512 to 4096 tokens; the last document holds 4096 tokens and ends at 32768.
All inputs are finite; a program needn't handle non-finite values.
Results may differ from the reference program's by a relative error of at most 0.014.
Values may be sent and summed in bfloat16 or wider, within the bound.
No kernel may reach another device: no remote copies, remote signals or barrier semaphores. Data moves between devices by JAX's collectives and lax.ppermute only.
A program may use at most 64 MiB of HBM per device.

```python
import jax
import jax.numpy as jnp
from jax import lax

Q_HEADS = 32
KV_HEADS = 8
D_HEAD = 128
BLOCK = 512
MAX_DOC = 4096
TOKENS = 32768
DOCS = 16


def draw_queries(key, part):
    key = jax.random.fold_in(key, 1)
    result = jnp.clip(jax.random.normal(key, (TOKENS, Q_HEADS, D_HEAD), jnp.float32), -6.0, 6.0)
    return result.reshape(TOKENS, Q_HEADS * D_HEAD).astype(jnp.bfloat16)


def draw_keys(key, part):
    key = jax.random.fold_in(key, 2)
    result = jnp.clip(jax.random.normal(key, (TOKENS, KV_HEADS, D_HEAD), jnp.float32), -6.0, 6.0)
    return result.reshape(TOKENS, KV_HEADS * D_HEAD).astype(jnp.bfloat16)


def draw_doc_starts(key, part):
    key = jax.random.fold_in(key, 5)
    slots = jnp.arange(DOCS)
    last_slot = DOCS - 1
    shares_weight = jax.random.randint(jax.random.fold_in(key, 1), (DOCS,), 60, 101)
    room = TOKENS - 2 * MAX_DOC - (DOCS - 2) * BLOCK
    if DOCS >= 4 and room >= BLOCK:
        long_slot = jax.random.randint(jax.random.fold_in(key, 2), (), 1, DOCS - 2)
        target = jax.random.randint(jax.random.fold_in(key, 3), (), 1, BLOCK)
        pinned = (slots == last_slot) | (slots == long_slot)
        shares_weight = jnp.where(pinned, 0, shares_weight)
        spare = room - BLOCK
        shares = spare * shares_weight // jnp.sum(shares_weight)
        leftover = spare - jnp.sum(shares)
        extra = jnp.where(slots == 0, leftover, 0)
        lengths = jnp.where(pinned, MAX_DOC, BLOCK + shares + extra)
        before = jnp.sum(jnp.where(slots < long_slot, lengths, 0))
        offset = (target - before) % BLOCK
        lengths = lengths + jnp.where(slots == long_slot - 1, offset, 0)
        lengths = lengths + jnp.where(slots == long_slot + 1, BLOCK - offset, 0)
    else:
        shares_weight = jnp.where(slots == last_slot, 0, shares_weight)
        spare = TOKENS - MAX_DOC - (DOCS - 1) * BLOCK
        shares = spare * shares_weight // jnp.sum(shares_weight)
        leftover = spare - jnp.sum(shares)
        extra = jnp.where(slots == 0, leftover, 0)
        lengths = jnp.where(slots == last_slot, MAX_DOC, BLOCK + shares + extra)
    return (jnp.cumsum(lengths) - lengths).astype(jnp.int32)


def block_scale(stream_key, dims, cuts, smallest, high):
    factor_of = 1.0
    for dim, parts in cuts:
        heights = jax.random.uniform(jax.random.fold_in(jax.random.fold_in(stream_key, 6), dim), (parts,), jnp.float32, smallest / len(cuts), high / len(cuts))
        factor_of = factor_of * jnp.repeat(jnp.exp(heights), dims[dim] // parts).reshape((-1,) + (1,) * (len(dims) - 1 - dim))
    return factor_of


def scatter_about(stream_key, dims, width, reach, shards=(), held_as=jnp.bfloat16):
    drawn = width * jax.random.normal(stream_key, dims, jnp.float32)
    if shards:
        drawn = drawn * block_scale(stream_key, dims, shards, -0.22, 0.18)
    return jnp.clip(drawn, -reach, reach).astype(held_as)


def setup_inputs(seed: int = 0) -> dict:
    arg_keys = jax.random.split(jax.random.key(seed), 5)
    queries = draw_queries(jax.random.fold_in(arg_keys[4], 71), 0)
    keys = draw_keys(jax.random.fold_in(arg_keys[4], 71), 0)
    values = scatter_about(arg_keys[2], (TOKENS, KV_HEADS * D_HEAD), 1.0, 6.0, ((0, 512),))
    doc_starts = draw_doc_starts(jax.random.fold_in(arg_keys[4], 71), 0)
    return {"queries": queries, "keys": keys, "values": values, "doc_starts": doc_starts}


FLOOR = -1.0e30


def doc_numbers(doc_starts, positions):
    return jnp.sum((doc_starts[None, :] <= positions[:, None]).astype(jnp.int32), axis=1) - 1


def reference(queries, keys, values, doc_starts):
    token_count = queries.shape[0]
    group_size = Q_HEADS // KV_HEADS
    window = MAX_DOC + BLOCK
    score_scale = D_HEAD ** -0.5
    positions = jnp.arange(token_count, dtype=jnp.int32)
    documents = doc_numbers(doc_starts, positions)
    pad_docs = jnp.concatenate([jnp.full((window,), -1, jnp.int32), documents])
    pad_positions = jnp.concatenate([jnp.arange(window, dtype=jnp.int32) - window, positions])
    pad_keys = jnp.concatenate([jnp.zeros((window, KV_HEADS * D_HEAD), keys.dtype), keys]).reshape(-1, KV_HEADS, D_HEAD)
    pad_values = jnp.concatenate([jnp.zeros((window, KV_HEADS * D_HEAD), values.dtype), values]).reshape(-1, KV_HEADS, D_HEAD)
    query_blocks = queries.reshape(token_count // BLOCK, BLOCK, KV_HEADS, group_size, D_HEAD)

    def one_block(inputs):
        q_block, block_number = inputs
        q_start = (block_number * BLOCK).astype(jnp.int32)
        k_start = q_start + BLOCK
        q_rows = q_block.astype(jnp.float32)
        k_rows = lax.dynamic_slice_in_dim(pad_keys, k_start, window, 0).astype(jnp.float32)
        v_rows = lax.dynamic_slice_in_dim(pad_values, k_start, window, 0).astype(jnp.float32)
        k_docs = lax.dynamic_slice_in_dim(pad_docs, k_start, window, 0)
        k_pos = lax.dynamic_slice_in_dim(pad_positions, k_start, window, 0)
        q_docs = lax.dynamic_slice_in_dim(documents, q_start, BLOCK, 0)
        q_pos = q_start + jnp.arange(BLOCK, dtype=jnp.int32)
        allowed = (q_docs[:, None] == k_docs[None, :]) & (k_pos[None, :] <= q_pos[:, None])
        scores = jnp.einsum("qhgd,khd->hgqk", q_rows, k_rows) * score_scale
        maxima = jnp.max(jnp.where(allowed, scores, FLOOR), axis=3)
        weights = jnp.where(allowed, jnp.exp(scores - maxima[..., None]), 0.0)
        totals = jnp.sum(weights, axis=3)
        mixed = jnp.einsum("hgqk,khd->hgqd", weights.astype(jnp.bfloat16).astype(jnp.float32), v_rows)
        result = mixed / totals[..., None]
        return jnp.transpose(result, (2, 0, 1, 3)).reshape(BLOCK, Q_HEADS * D_HEAD).astype(jnp.bfloat16)

    numbers = jnp.arange(token_count // BLOCK, dtype=jnp.int32)
    blocks_out = lax.map(one_block, (query_blocks, numbers))
    return blocks_out.reshape(token_count, Q_HEADS * D_HEAD)
```

```python
import functools
import math

import jax
import jax.numpy as jnp
from jax import lax
from jax.experimental import pallas as pl
from jax.experimental.pallas import tpu as pltpu
from jax.sharding import Mesh, PartitionSpec as P

D_HEAD = 128
BLOCK = 512
MAX_DOC = 4096
PLANE = 32
ROW = 8
SUPER = 2 * BLOCK
SLOTS = (MAX_DOC + SUPER) // BLOCK
FLOOR = -1.0e30
SCALE = D_HEAD**-0.5 * math.log2(math.e)
PART = 128
ROWS = 2 * BLOCK


def attend(late, starts, q_ref, *refs):
    if late:
        z2, yb, yac, xb, xc, acc_in, top_in, out_ref = refs[:8]
    else:
        own, z1, xa, acc_out, top_out = refs[:5]
    (k_ref, v_ref, qx_ref, scores_a, scores_b, weights, acc, top_ref, shift,
     k_sem, v_sem) = refs[-11:]
    me = lax.axis_index("d")
    z = me // PLANE
    pair = lax.rem(me // (2 * ROW), 2)
    core = lax.rem(me, 2)
    s_first = (z * 2 + pair) * SUPER

    firsts, lasts, counts = [], [], []
    for pos in range(2):
        q_start = s_first + pos * BLOCK
        first = jnp.int32(0)
        last = jnp.int32(0)
        for i in range(starts.shape[0]):
            s = starts[i]
            first = jnp.where(s <= q_start, s, first)
            last = jnp.where(s <= q_start + BLOCK - 1, s, last)
        firsts.append(first)
        lasts.append(last)
        counts.append((q_start - first + BLOCK - 1) // BLOCK)
    lowest = jnp.minimum(SLOTS - 2 - counts[0], SLOTS - 1 - counts[1])

    def fetch(j, mine, mine_row, other, other_row, when):
        swapped = lax.rem(pair + j, 2)
        for half in range(2):
            slot = SLOTS - 2 - 2 * j + lax.bitwise_xor(half, swapped)
            to = pl.ds(pl.multiple_of(slot * BLOCK, BLOCK), BLOCK)
            for c in range(2):
                @pl.when((core == c) & (slot >= lowest) & when)
                def _():
                    mine_at = mine.at[pl.ds(mine_row + half * BLOCK, BLOCK)]
                    other_at = other.at[pl.ds(other_row + half * BLOCK, BLOCK)]
                    k_src, v_src = (mine_at, other_at) if c == 0 else (other_at, mine_at)
                    pltpu.make_async_copy(k_src, k_ref.at[to, 0:D_HEAD], k_sem.at[slot]).start()
                    pltpu.make_async_copy(v_src, v_ref.at[to, 0:D_HEAD], v_sem.at[slot]).start()

    always = me >= 0
    if late:
        fetch(1, yac, 0, xc, 0, pair == 1)
        fetch(1, yb, 0, xb, SUPER, pair == 0)
        fetch(3, yb, 0, xb, SUPER, pair == 1)
        fetch(3, yac, 0, xc, 0, pair == 0)
        fetch(4, z2, 0, xb, 0, always)
        ranges = ((0, 4), (6, 8))
        any_block = z2
    else:
        fetch(0, own, 0, xa, 0, always)
        fetch(2, z1, 0, xa, SUPER, always)
        ranges = ((4, 6), (8, 10))
        any_block = own

    lane = lax.broadcasted_iota(jnp.int32, (BLOCK, D_HEAD), 1)
    row = lax.broadcasted_iota(jnp.int32, (BLOCK, D_HEAD), 0)
    limits = jnp.where(lane == 0, firsts[0], jnp.where(lane == 1, firsts[1],
                       jnp.where(lane == 2, lasts[0], jnp.where(lane == 3, lasts[1], 0))))
    base = s_first - (SLOTS - 2) * BLOCK
    behind = limits - row - base

    def bias(slot, carry):
        to = pl.ds(pl.multiple_of(slot * BLOCK, BLOCK), BLOCK)
        ahead = behind > slot * BLOCK
        k_ref[to, D_HEAD:] = jnp.where(ahead, FLOOR, 0.0).astype(jnp.bfloat16)
        v_ref[to, D_HEAD:] = jnp.ones((BLOCK, D_HEAD), jnp.bfloat16)
        return carry

    def arrive(slot, carry):
        to = pl.ds(pl.multiple_of(slot * BLOCK, BLOCK), BLOCK)
        rows = pl.ds(0, BLOCK)
        pltpu.make_async_copy(any_block.at[rows], k_ref.at[to, 0:D_HEAD], k_sem.at[slot]).wait()
        pltpu.make_async_copy(any_block.at[rows], v_ref.at[to, 0:D_HEAD], v_sem.at[slot]).wait()
        return carry

    for low, high in ranges:
        lax.fori_loop(jnp.maximum(lowest, low), high, bias, 0)

    groups = [slice(g, g + D_HEAD) for g in range(0, BLOCK, D_HEAD)]
    parts = [slice(r, r + PART) for r in range(0, ROWS, PART)]

    class Tile:
        def __init__(self, half):
            self.half = half
            self.scores = scores_b if half else scores_a
            pos = lax.bitwise_xor(half, pair)
            self.own = SLOTS - 2 + pos
            n = jnp.where(pos == 0, counts[0], counts[1])
            border = jnp.where(pos == 0, lasts[0], lasts[1]) - s_first - pos * BLOCK
            column = jnp.where(row >= border, pos + 2, pos)
            marks = jnp.where((lane == pos) | (lane == column), 1.0, 0.0).astype(jnp.bfloat16)
            for head in range(2):
                to = slice(head * BLOCK, (head + 1) * BLOCK)
                at = slice(head * D_HEAD, (head + 1) * D_HEAD)
                qx_ref[half, to, 0:D_HEAD] = q_ref[half * BLOCK:(half + 1) * BLOCK, at]
                qx_ref[half, to, D_HEAD:] = marks
            m = n - pos
            if late:
                self.steps = jnp.clip(m, 0, 2) + jnp.clip(m - 4, 0, 4)
                self.distance = lambda i: jnp.where(i < 2, i + 1, i + 3) + pos
            else:
                beside = jnp.where((pos == 1) & (n >= 1), 1, 0)
                self.steps = beside + jnp.clip(m - 2, 0, 2)
                self.distance = lambda i: jnp.where((pos == 1) & (i == 0), 1, i + 3)

        def keys(self, d):
            return pl.ds(pl.multiple_of((self.own - d) * BLOCK, BLOCK), BLOCK)

        def weigh(self, b, d):
            for r in parts:
                for g in groups:
                    p = jnp.exp2(self.scores[b, r, g] * SCALE - shift[r, :])
                    weights[r, g] = p.astype(jnp.bfloat16)
            return jnp.dot(weights[...], v_ref[self.keys(d), :], preferred_element_type=jnp.float32)

        def fresh(self, b, d):
            self.scores[b] = lax.dot_general(
                qx_ref[self.half], k_ref[self.keys(d), :], (((1,), (1,)), ((), ())),
                preferred_element_type=jnp.float32)
            for r in parts:
                top = top_ref[r, :]
                query = slice(r.start % BLOCK, r.start % BLOCK + PART)
                for g in groups:
                    part = self.scores[b, r, g]
                    if isinstance(d, int):
                        part = jnp.where(lane[query] + g.start <= row[query], part, FLOOR)
                        self.scores[b, r, g] = part
                    top = jnp.maximum(top, part)
                top_ref[r, :] = top

    def loop(first, stop, old, young):
        def go(i, carry):
            b = i if late else i + 1
            if old:
                acc[...] += old.weigh(b, old.distance(i))
            if young:
                young.fresh(b, young.distance(i))
            return carry

        lax.fori_loop(first, stop, go, 0)

    tiles = [Tile(half) for half in range(2)]
    for low, high in ranges:
        lax.fori_loop(jnp.maximum(lowest, low), high, arrive, 0)
    for t in range(3):
        cur = tiles[t - 1] if t > 0 else None
        new = tiles[t] if t < 2 else None
        if cur and not late:
            acc[...] = cur.weigh(0, 0)
        if new and late:
            top_ref[...] = top_in[new.half]
        elif new:
            top_ref[...] = jnp.full((ROWS, D_HEAD), FLOOR, jnp.float32)
            new.fresh(0, 0)
        if cur and new:
            both = jnp.minimum(cur.steps, new.steps)
            loop(0, both, cur, new)
            loop(both, cur.steps, cur, None)
            loop(both, new.steps, None, new)
        elif cur:
            loop(0, cur.steps, cur, None)
        else:
            loop(0, new.steps, None, new)
        if cur and late:
            for head in range(2):
                r = slice(head * BLOCK, (head + 1) * BLOCK)
                mixed = acc[r, 0:D_HEAD] / acc[r, D_HEAD:]
                out_ref[cur.half * BLOCK:(cur.half + 1) * BLOCK,
                        head * D_HEAD:(head + 1) * D_HEAD] = mixed.astype(jnp.bfloat16)
        elif cur:
            acc_out[cur.half] = acc[...]
        if new:
            for r in parts:
                top = jnp.max(top_ref[r, :], axis=1, keepdims=True)
                top = jnp.broadcast_to(top, (PART, D_HEAD))
                shift[r, :] = top * SCALE
                if late:
                    rescale = jnp.exp2((top_in[new.half, r, :] - top) * SCALE)
                    acc[r, 0:D_HEAD] = acc_in[new.half, r, 0:D_HEAD] * rescale
                    acc[r, D_HEAD:] = acc_in[new.half, r, D_HEAD:] * rescale
                else:
                    top_out[new.half, r, :] = top


def attention(late, doc_starts, q, blocks, state=()):
    vmem = pl.BlockSpec(memory_space=pltpu.VMEM)
    if late:
        out_shape, out_specs = jax.ShapeDtypeStruct(q.shape, jnp.bfloat16), vmem
    else:
        out_shape = (jax.ShapeDtypeStruct((2, ROWS, 2 * D_HEAD), jnp.float32),
                     jax.ShapeDtypeStruct((2, ROWS, D_HEAD), jnp.float32))
        out_specs = (vmem,) * 2
    scores = pltpu.VMEM((6 if late else 4, ROWS, BLOCK), jnp.float32)
    return pl.pallas_call(
        functools.partial(attend, late),
        out_shape=out_shape,
        in_specs=[pl.BlockSpec(memory_space=pltpu.SMEM), vmem]
        + [pl.BlockSpec(memory_space=pl.ANY)] * len(blocks) + [vmem] * len(state),
        out_specs=out_specs,
        scratch_shapes=[
            pltpu.VMEM((SLOTS * BLOCK, 2 * D_HEAD), jnp.bfloat16),
            pltpu.VMEM((SLOTS * BLOCK, 2 * D_HEAD), jnp.bfloat16),
            pltpu.VMEM((2, ROWS, 2 * D_HEAD), jnp.bfloat16),
            scores,
            scores,
            pltpu.VMEM((ROWS, BLOCK), jnp.bfloat16),
            pltpu.VMEM((ROWS, 2 * D_HEAD), jnp.float32),
            pltpu.VMEM((ROWS, D_HEAD), jnp.float32),
            pltpu.VMEM((ROWS, D_HEAD), jnp.float32),
            pltpu.SemaphoreType.DMA((SLOTS,)),
            pltpu.SemaphoreType.DMA((SLOTS,)),
        ],
        compiler_params=pltpu.CompilerParams(vmem_limit_bytes=44 * 1024 * 1024),
        cost_estimate=pl.CostEstimate(
            flops=(3 if late else 2) * 10**9, bytes_accessed=4 * 10**6, transcendentals=3 * 10**6
        ),
        name="late_blocks" if late else "early_blocks",
    )(doc_starts, q, *blocks, *state)


def per_device(queries, keys, values, doc_starts):
    devices = lax.axis_size("d")
    rows = queries.shape[0]
    groups = []
    for z in range(0, devices, PLANE):
        groups.append(list(range(z, z + 16)))
        groups.append(list(range(z + 24, z + 32)) + list(range(z + 16, z + 24)))

    def exchange(x):
        return lax.all_to_all(
            x, "d", split_axis=0, concat_axis=0, axis_index_groups=groups, tiled=True
        )

    def move(x, rule):
        pairs = []
        for d in range(devices):
            z, y = d // PLANE, d // ROW % 4
            to = rule(d, z, y)
            if to is not None and to < devices:
                pairs.append((d, to))
        return lax.ppermute(x, "d", pairs)

    def mirror(d, y):
        return d + ROW * (3 - 2 * y)

    def cores(x):
        return move(x, lambda d, z, y: d ^ 1)

    heads = keys.shape[1] // D_HEAD
    kv = jnp.stack(
        [keys.reshape(rows, heads, D_HEAD), values.reshape(rows, heads, D_HEAD)], axis=2
    ).reshape(rows, 2 * heads, D_HEAD).transpose(1, 0, 2)
    own = exchange(kv).reshape(SUPER, D_HEAD)
    q = queries.reshape(rows, 2 * heads, 2 * D_HEAD).transpose(1, 0, 2)
    q = exchange(q).reshape(SUPER, 2 * D_HEAD)

    first_pair = (lax.axis_index("d") & (2 * ROW)) == 0
    z1 = move(own, lambda d, z, y: d + PLANE)
    z2 = move(z1, lambda d, z, y: d + PLANE if z > 0 else None)
    yb = move(z1, lambda d, z, y: mirror(d, y))
    xa = cores(jnp.concatenate([own, z1]))
    z2, q = lax.optimization_barrier((z2, q))
    yac = move(jnp.where(first_pair, own, z2), lambda d, z, y: mirror(d, y))
    xb = cores(jnp.concatenate([z2, yb]))
    state = attention(False, doc_starts, q, (own, z1, xa))
    yac, state = lax.optimization_barrier((yac, state))
    xc = cores(yac)
    out = attention(True, doc_starts, q, (z2, yb, yac, xb, xc), state)
    out = exchange(out.reshape(2 * heads, rows, 2 * D_HEAD))
    return out.transpose(1, 0, 2).reshape(rows, heads * 4 * D_HEAD)


def solution(mesh):
    mesh = Mesh(mesh.devices.reshape(-1), ("d",))
    rows = P("d", None)
    return jax.shard_map(
        per_device, mesh=mesh, in_specs=(rows, rows, rows, P()), out_specs=rows, check_vma=False
    )
```

```python
import functools
import math

import jax
import jax.numpy as jnp
from jax import lax
from jax.experimental import pallas as pl
from jax.experimental.pallas import tpu as pltpu
from jax.sharding import Mesh, PartitionSpec as P

D_HEAD = 128
BLOCK = 512
MAX_DOC = 4096
PLANE = 32
ROW = 8
SUPER = 2 * BLOCK
SLOTS = (MAX_DOC + SUPER) // BLOCK
FLOOR = -1.0e30
SCALE = D_HEAD**-0.5 * math.log2(math.e)
PART = 128
PIECE = BLOCK // 2
ROWS = 2 * BLOCK


def attend(late, starts, q_ref, *refs):
    if late:
        z2, yb, yac, xb, xc, acc_in, top_in, out_ref = refs[:8]
    else:
        own, z1, xa, acc_out, top_out = refs[:5]
    (k_ref, v_ref, qx_ref, scores_a, scores_b, weights, acc, top_ref, shift,
     k_sem, v_sem) = refs[-11:]
    me = lax.axis_index("d")
    z = me // PLANE
    pair = lax.rem(me // (2 * ROW), 2)
    core = lax.rem(me, 2)
    s_first = (z * 2 + pair) * SUPER

    firsts, lasts, counts = [], [], []
    for pos in range(2):
        q_start = s_first + pos * BLOCK
        first = jnp.int32(0)
        last = jnp.int32(0)
        for i in range(starts.shape[0]):
            s = starts[i]
            first = jnp.where(s <= q_start, s, first)
            last = jnp.where(s <= q_start + BLOCK - 1, s, last)
        firsts.append(first)
        lasts.append(last)
        counts.append((q_start - first + BLOCK - 1) // BLOCK)
    lowest = jnp.minimum(SLOTS - 2 - counts[0], SLOTS - 1 - counts[1])

    def fetch(j, mine, mine_row, other, other_row, when):
        swapped = lax.rem(pair + j, 2)
        for half in range(2):
            slot = SLOTS - 2 - 2 * j + lax.bitwise_xor(half, swapped)
            to = pl.ds(pl.multiple_of(slot * BLOCK, BLOCK), BLOCK)
            for c in range(2):
                @pl.when((core == c) & (slot >= lowest) & when)
                def _():
                    mine_at = mine.at[pl.ds(mine_row + half * BLOCK, BLOCK)]
                    other_at = other.at[pl.ds(other_row + half * BLOCK, BLOCK)]
                    k_src, v_src = (mine_at, other_at) if c == 0 else (other_at, mine_at)
                    pltpu.make_async_copy(k_src, k_ref.at[to, 0:D_HEAD], k_sem.at[slot]).start()
                    pltpu.make_async_copy(v_src, v_ref.at[to, 0:D_HEAD], v_sem.at[slot]).start()

    always = me >= 0
    if late:
        fetch(1, yac, 0, xc, 0, pair == 1)
        fetch(1, yb, 0, xb, SUPER, pair == 0)
        fetch(3, yb, 0, xb, SUPER, pair == 1)
        fetch(3, yac, 0, xc, 0, pair == 0)
        fetch(4, z2, 0, xb, 0, always)
        ranges = ((0, 4), (6, 8))
        any_block = z2
    else:
        fetch(0, own, 0, xa, 0, always)
        fetch(2, z1, 0, xa, SUPER, always)
        ranges = ((4, 6), (8, 10))
        any_block = own

    lane = lax.broadcasted_iota(jnp.int32, (BLOCK, D_HEAD), 1)
    row = lax.broadcasted_iota(jnp.int32, (BLOCK, D_HEAD), 0)
    limits = jnp.where(lane == 0, firsts[0], jnp.where(lane == 1, firsts[1],
                       jnp.where(lane == 2, lasts[0], jnp.where(lane == 3, lasts[1], 0))))
    base = s_first - (SLOTS - 2) * BLOCK
    behind = limits - row - base

    def bias(slot, carry):
        to = pl.ds(pl.multiple_of(slot * BLOCK, BLOCK), BLOCK)
        ahead = behind > slot * BLOCK
        k_ref[to, D_HEAD:] = jnp.where(ahead, FLOOR, 0.0).astype(jnp.bfloat16)
        v_ref[to, D_HEAD:] = jnp.ones((BLOCK, D_HEAD), jnp.bfloat16)
        return carry

    def arrive(slot, carry):
        to = pl.ds(pl.multiple_of(slot * BLOCK, BLOCK), BLOCK)
        rows = pl.ds(0, BLOCK)
        pltpu.make_async_copy(any_block.at[rows], k_ref.at[to, 0:D_HEAD], k_sem.at[slot]).wait()
        pltpu.make_async_copy(any_block.at[rows], v_ref.at[to, 0:D_HEAD], v_sem.at[slot]).wait()
        return carry

    for low, high in ranges:
        lax.fori_loop(jnp.maximum(lowest, low), high, bias, 0)

    groups = [slice(g, g + D_HEAD) for g in range(0, BLOCK, D_HEAD)]
    parts = [slice(r, r + PART) for r in range(0, ROWS, PART)]

    def pieces(half):
        for i in range(4):
            part, head = divmod(i, 2)
            first = half * BLOCK + part * PIECE
            yield (slice(i * PIECE, (i + 1) * PIECE), slice(first, first + PIECE),
                   slice(head * D_HEAD, (head + 1) * D_HEAD))

    class Tile:
        def __init__(self, half):
            self.half = half
            self.scores = scores_b if half else scores_a
            pos = lax.bitwise_xor(half, pair)
            self.own = SLOTS - 2 + pos
            n = jnp.where(pos == 0, counts[0], counts[1])
            border = jnp.where(pos == 0, lasts[0], lasts[1]) - s_first - pos * BLOCK
            column = jnp.where(row >= border, pos + 2, pos)
            marks = jnp.where((lane == pos) | (lane == column), 1.0, 0.0).astype(jnp.bfloat16)
            for rows, tokens, columns in pieces(half):
                qx_ref[half, rows, 0:D_HEAD] = q_ref[tokens, columns]
                query = tokens.start % BLOCK
                qx_ref[half, rows, D_HEAD:] = marks[query:query + PIECE]
            m = n - pos
            if late:
                self.steps = jnp.clip(m, 0, 2) + jnp.clip(m - 4, 0, 4)
                self.distance = lambda i: jnp.where(i < 2, i + 1, i + 3) + pos
            else:
                beside = jnp.where((pos == 1) & (n >= 1), 1, 0)
                self.steps = beside + jnp.clip(m - 2, 0, 2)
                self.distance = lambda i: jnp.where((pos == 1) & (i == 0), 1, i + 3)

        def keys(self, d, first=0, size=BLOCK):
            return pl.ds(pl.multiple_of((self.own - d) * BLOCK + first, PIECE), size)

        def score(self, d, rows=slice(None), first=0, size=BLOCK):
            return lax.dot_general(
                qx_ref[self.half, rows], k_ref[self.keys(d, first, size), :],
                (((1,), (1,)), ((), ())), preferred_element_type=jnp.float32)

        def mix(self, d, rows=slice(None), first=0, size=BLOCK, at=0):
            return jnp.dot(weights[rows, at + first:at + first + size],
                           v_ref[self.keys(d, first, size), :], preferred_element_type=jnp.float32)

        def exponents(self, b, at=0, diagonal=False):
            for r in parts:
                for g in groups:
                    if diagonal and r.start < BLOCK and g.start >= PIECE:
                        continue
                    p = jnp.exp2(self.scores[b, r, g] * SCALE - shift[r, :])
                    weights[r, at + g.start:at + g.stop] = p.astype(jnp.bfloat16)

        def tops(self, blocks, diagonal=False):
            for r in parts:
                top = top_ref[r, :]
                query = r.start // BLOCK * PIECE + r.start % PIECE
                query = slice(query, query + PART)
                for b in blocks:
                    for g in groups:
                        if diagonal and r.start < BLOCK and g.start >= PIECE:
                            continue
                        part = self.scores[b, r, g]
                        if diagonal:
                            part = jnp.where(lane[query] + g.start <= row[query], part, FLOOR)
                            self.scores[b, r, g] = part
                        top = jnp.maximum(top, part)
                top_ref[r, :] = top

        def weigh(self, i, blocks):
            for j in range(blocks):
                self.exponents(i + j if late else i + j + 1, j * BLOCK)
            product = self.mix(self.distance(i))
            for j in range(1, blocks):
                product += self.mix(self.distance(i + j), at=j * BLOCK)
            acc[...] += product

        def fresh(self, i, blocks):
            buffers = [i + j if late else i + j + 1 for j in range(blocks)]
            for j in range(blocks):
                self.scores[buffers[j]] = self.score(self.distance(i + j))
            self.tops(buffers)

        def weigh_own(self):
            self.exponents(0, diagonal=True)
            acc[...] = self.mix(0, size=PIECE)
            acc[BLOCK:, :] += self.mix(0, rows=slice(BLOCK, ROWS), first=PIECE, size=PIECE)

        def fresh_own(self):
            self.scores[0, :, 0:PIECE] = self.score(0, size=PIECE)
            self.scores[0, BLOCK:, PIECE:] = self.score(0, slice(BLOCK, ROWS), PIECE, PIECE)
            self.tops([0], diagonal=True)

    def loop(first, stop, old, young):
        def go(i, blocks):
            if old:
                old.weigh(i, blocks)
            if young:
                young.fresh(i, blocks)

        def two(i, carry):
            go(first + 2 * i, 2)
            return carry

        def one(i, carry):
            go(i, 1)
            return carry

        twos = (stop - first) // 2
        lax.fori_loop(0, twos, two, 0)
        lax.fori_loop(first + 2 * twos, stop, one, 0)

    tiles = [Tile(half) for half in range(2)]
    for low, high in ranges:
        lax.fori_loop(jnp.maximum(lowest, low), high, arrive, 0)
    for t in range(3):
        cur = tiles[t - 1] if t > 0 else None
        new = tiles[t] if t < 2 else None
        if cur and not late:
            cur.weigh_own()
        if new and late:
            top_ref[...] = top_in[new.half]
        elif new:
            top_ref[...] = jnp.full((ROWS, D_HEAD), FLOOR, jnp.float32)
            new.fresh_own()
        if cur and new:
            both = jnp.minimum(cur.steps, new.steps)
            loop(0, both, cur, new)
            loop(both, cur.steps, cur, None)
            loop(both, new.steps, None, new)
        elif cur:
            loop(0, cur.steps, cur, None)
        else:
            loop(0, new.steps, None, new)
        if cur and late:
            for rows, tokens, columns in pieces(cur.half):
                mixed = acc[rows, 0:D_HEAD] / acc[rows, D_HEAD:]
                out_ref[tokens, columns] = mixed.astype(jnp.bfloat16)
        elif cur:
            acc_out[cur.half] = acc[...]
        if new:
            for r in parts:
                top = jnp.max(top_ref[r, :], axis=1, keepdims=True)
                top = jnp.broadcast_to(top, (PART, D_HEAD))
                shift[r, :] = top * SCALE
                if late:
                    rescale = jnp.exp2((top_in[new.half, r, :] - top) * SCALE)
                    acc[r, 0:D_HEAD] = acc_in[new.half, r, 0:D_HEAD] * rescale
                    acc[r, D_HEAD:] = acc_in[new.half, r, D_HEAD:] * rescale
                else:
                    top_out[new.half, r, :] = top


def pack(keys, values, out, sems):
    copies = []
    for i in range(out.shape[0]):
        head, part = divmod(i, 2)
        source = (keys, values)[part].at[:, head * D_HEAD:(head + 1) * D_HEAD]
        copies.append(pltpu.make_async_copy(source, out.at[i], sems.at[i]))
        copies[-1].start()
    for copy in copies:
        copy.wait()


def attention(late, doc_starts, q, blocks, state=()):
    vmem = pl.BlockSpec(memory_space=pltpu.VMEM)
    if late:
        out_shape, out_specs = jax.ShapeDtypeStruct(q.shape, jnp.bfloat16), vmem
    else:
        out_shape = (jax.ShapeDtypeStruct((2, ROWS, 2 * D_HEAD), jnp.float32),
                     jax.ShapeDtypeStruct((2, ROWS, D_HEAD), jnp.float32))
        out_specs = (vmem,) * 2
    scores = pltpu.VMEM((6 if late else 4, ROWS, BLOCK), jnp.float32)
    return pl.pallas_call(
        functools.partial(attend, late),
        out_shape=out_shape,
        in_specs=[pl.BlockSpec(memory_space=pltpu.SMEM), vmem]
        + [pl.BlockSpec(memory_space=pl.ANY)] * len(blocks) + [vmem] * len(state),
        out_specs=out_specs,
        scratch_shapes=[
            pltpu.VMEM((SLOTS * BLOCK, 2 * D_HEAD), jnp.bfloat16),
            pltpu.VMEM((SLOTS * BLOCK, 2 * D_HEAD), jnp.bfloat16),
            pltpu.VMEM((2, ROWS, 2 * D_HEAD), jnp.bfloat16),
            scores,
            scores,
            pltpu.VMEM((ROWS, 2 * BLOCK), jnp.bfloat16),
            pltpu.VMEM((ROWS, 2 * D_HEAD), jnp.float32),
            pltpu.VMEM((ROWS, D_HEAD), jnp.float32),
            pltpu.VMEM((ROWS, D_HEAD), jnp.float32),
            pltpu.SemaphoreType.DMA((SLOTS,)),
            pltpu.SemaphoreType.DMA((SLOTS,)),
        ],
        compiler_params=pltpu.CompilerParams(vmem_limit_bytes=(44 if late else 36) * 1024 * 1024),
        cost_estimate=pl.CostEstimate(
            flops=(3 if late else 2) * 10**9, bytes_accessed=4 * 10**6, transcendentals=3 * 10**6
        ),
        name="late_blocks" if late else "early_blocks",
    )(doc_starts, q, *blocks, *state)


def per_device(queries, keys, values, doc_starts):
    devices = lax.axis_size("d")
    rows = queries.shape[0]
    groups = []
    for z in range(0, devices, PLANE):
        groups.append(list(range(z, z + 16)))
        groups.append(list(range(z + 24, z + 32)) + list(range(z + 16, z + 24)))

    def exchange(x):
        return lax.all_to_all(
            x, "d", split_axis=0, concat_axis=0, axis_index_groups=groups, tiled=True
        )

    def move(x, rule):
        pairs = []
        for d in range(devices):
            z, y = d // PLANE, d // ROW % 4
            to = rule(d, z, y)
            if to is not None and to < devices:
                pairs.append((d, to))
        return lax.ppermute(x, "d", pairs)

    def mirror(d, y):
        return d + ROW * (3 - 2 * y)

    def cores(x):
        return move(x, lambda d, z, y: d ^ 1)

    heads = keys.shape[1] // D_HEAD
    kv = pl.pallas_call(
        pack,
        out_shape=jax.ShapeDtypeStruct((2 * heads, rows, D_HEAD), keys.dtype),
        in_specs=[pl.BlockSpec(memory_space=pl.ANY)] * 2,
        out_specs=pl.BlockSpec(memory_space=pltpu.VMEM),
        scratch_shapes=[pltpu.SemaphoreType.DMA((2 * heads,))],
        compiler_params=pltpu.CompilerParams(vmem_limit_bytes=60 * 1024 * 1024),
        name="pack",
    )(keys, values)
    own = exchange(kv).reshape(SUPER, D_HEAD)
    q = queries.reshape(rows, 2 * heads, 2 * D_HEAD).transpose(1, 0, 2)
    q = exchange(q).reshape(SUPER, 2 * D_HEAD)

    first_pair = (lax.axis_index("d") & (2 * ROW)) == 0
    z1 = move(own, lambda d, z, y: d + PLANE)
    z2 = move(z1, lambda d, z, y: d + PLANE if z > 0 else None)
    yb = move(z1, lambda d, z, y: mirror(d, y))
    xa = cores(jnp.concatenate([own, z1]))
    z2, q = lax.optimization_barrier((z2, q))
    yac = move(jnp.where(first_pair, own, z2), lambda d, z, y: mirror(d, y))
    xb = cores(jnp.concatenate([z2, yb]))
    state = attention(False, doc_starts, q, (own, z1, xa))
    yac, state = lax.optimization_barrier((yac, state))
    xc = cores(yac)
    out = attention(True, doc_starts, q, (z2, yb, yac, xb, xc), state)
    out = exchange(out.reshape(2 * heads, rows, 2 * D_HEAD))
    return out.transpose(1, 0, 2).reshape(rows, heads * 4 * D_HEAD)


def solution(mesh):
    mesh = Mesh(mesh.devices.reshape(-1), ("d",))
    rows = P("d", None)
    return jax.shard_map(
        per_device, mesh=mesh, in_specs=(rows, rows, rows, P()), out_specs=rows, check_vma=False
    )
```

```python
import functools
import math

import jax
import jax.numpy as jnp
from jax import lax
from jax.experimental import pallas as pl
from jax.experimental.pallas import tpu as pltpu
from jax.sharding import Mesh, PartitionSpec as P

D_HEAD = 128
BLOCK = 512
MAX_DOC = 4096
PLANE = 32
ROW = 8
SUPER = 2 * BLOCK
SLOTS = (MAX_DOC + SUPER) // BLOCK
FLOOR = -1.0e30
SCALE = D_HEAD**-0.5 * math.log2(math.e)
PART = 128
PIECE = BLOCK // 2
ROWS = 2 * BLOCK


def attend(late, starts, q_ref, *refs):
    if late:
        z2, yb, yac, xb, xc, acc_in, top_in, out_ref = refs[:8]
    else:
        own, z1, xa, acc_out, top_out = refs[:5]
    (k_ref, v_ref, qx_ref, scores_a, scores_b, weights, acc, top_ref, shift,
     k_sem, v_sem) = refs[-11:]
    me = lax.axis_index("d")
    z = me // PLANE
    pair = lax.rem(me // (2 * ROW), 2)
    core = lax.rem(me, 2)
    s_first = (z * 2 + pair) * SUPER

    firsts, lasts, counts = [], [], []
    for pos in range(2):
        q_start = s_first + pos * BLOCK
        first = jnp.int32(0)
        last = jnp.int32(0)
        for i in range(starts.shape[0]):
            s = starts[i]
            first = jnp.where(s <= q_start, s, first)
            last = jnp.where(s <= q_start + BLOCK - 1, s, last)
        firsts.append(first)
        lasts.append(last)
        counts.append((q_start - first + BLOCK - 1) // BLOCK)
    lowest = jnp.minimum(SLOTS - 2 - counts[0], SLOTS - 1 - counts[1])

    def fetch(j, mine, mine_row, other, other_row, when):
        swapped = lax.rem(pair + j, 2)
        for half in range(2):
            slot = SLOTS - 2 - 2 * j + lax.bitwise_xor(half, swapped)
            to = pl.ds(pl.multiple_of(slot * BLOCK, BLOCK), BLOCK)
            for c in range(2):
                @pl.when((core == c) & (slot >= lowest) & when)
                def _():
                    mine_at = mine.at[pl.ds(mine_row + half * BLOCK, BLOCK)]
                    other_at = other.at[pl.ds(other_row + half * BLOCK, BLOCK)]
                    k_src, v_src = (mine_at, other_at) if c == 0 else (other_at, mine_at)
                    pltpu.make_async_copy(k_src, k_ref.at[to, 0:D_HEAD], k_sem.at[slot]).start()
                    pltpu.make_async_copy(v_src, v_ref.at[to, 0:D_HEAD], v_sem.at[slot]).start()

    always = me >= 0
    if late:
        fetch(1, yac, 0, xc, 0, pair == 1)
        fetch(1, yb, 0, xb, SUPER, pair == 0)
        fetch(3, yb, 0, xb, SUPER, pair == 1)
        fetch(3, yac, 0, xc, 0, pair == 0)
        fetch(4, z2, 0, xb, 0, always)
        ranges = ((0, 4), (6, 8))
        any_block = z2
    else:
        fetch(0, own, 0, xa, 0, always)
        fetch(2, z1, 0, xa, SUPER, always)
        ranges = ((4, 6), (8, 10))
        any_block = own

    lane = lax.broadcasted_iota(jnp.int32, (BLOCK, D_HEAD), 1)
    row = lax.broadcasted_iota(jnp.int32, (BLOCK, D_HEAD), 0)
    limits = jnp.where(lane == 0, firsts[0], jnp.where(lane == 1, firsts[1],
                       jnp.where(lane == 2, lasts[0], jnp.where(lane == 3, lasts[1], 0))))
    base = s_first - (SLOTS - 2) * BLOCK
    behind = limits - row - base

    def bias(slot, carry):
        to = pl.ds(pl.multiple_of(slot * BLOCK, BLOCK), BLOCK)
        ahead = behind > slot * BLOCK
        k_ref[to, D_HEAD:] = jnp.where(ahead, FLOOR, 0.0).astype(jnp.bfloat16)
        v_ref[to, D_HEAD:] = jnp.ones((BLOCK, D_HEAD), jnp.bfloat16)
        return carry

    def arrive(slot, carry):
        to = pl.ds(pl.multiple_of(slot * BLOCK, BLOCK), BLOCK)
        rows = pl.ds(0, BLOCK)
        pltpu.make_async_copy(any_block.at[rows], k_ref.at[to, 0:D_HEAD], k_sem.at[slot]).wait()
        pltpu.make_async_copy(any_block.at[rows], v_ref.at[to, 0:D_HEAD], v_sem.at[slot]).wait()
        return carry

    for low, high in ranges:
        lax.fori_loop(jnp.maximum(lowest, low), high, bias, 0)

    groups = [slice(g, g + D_HEAD) for g in range(0, BLOCK, D_HEAD)]
    parts = [slice(r, r + PART) for r in range(0, ROWS, PART)]

    def pieces(half):
        for i in range(4):
            part, head = divmod(i, 2)
            first = half * BLOCK + part * PIECE
            yield (slice(i * PIECE, (i + 1) * PIECE), slice(first, first + PIECE),
                   slice(head * D_HEAD, (head + 1) * D_HEAD))

    class Tile:
        def __init__(self, half):
            self.half = half
            self.scores = scores_b if half else scores_a
            pos = lax.bitwise_xor(half, pair)
            self.own = SLOTS - 2 + pos
            n = jnp.where(pos == 0, counts[0], counts[1])
            border = jnp.where(pos == 0, lasts[0], lasts[1]) - s_first - pos * BLOCK
            column = jnp.where(row >= border, pos + 2, pos)
            marks = jnp.where((lane == pos) | (lane == column), 1.0, 0.0).astype(jnp.bfloat16)
            for rows, tokens, columns in pieces(half):
                qx_ref[half, rows, 0:D_HEAD] = q_ref[tokens, columns]
                query = tokens.start % BLOCK
                qx_ref[half, rows, D_HEAD:] = marks[query:query + PIECE]
            m = n - pos
            if late:
                self.steps = jnp.clip(m, 0, 2) + jnp.clip(m - 4, 0, 4)
                self.distance = lambda i: jnp.where(i < 2, i + 1, i + 3) + pos
            else:
                beside = jnp.where((pos == 1) & (n >= 1), 1, 0)
                self.steps = beside + jnp.clip(m - 2, 0, 2)
                self.distance = lambda i: jnp.where((pos == 1) & (i == 0), 1, i + 3)

        def keys(self, d, first=0, size=BLOCK):
            return pl.ds(pl.multiple_of((self.own - d) * BLOCK + first, PIECE), size)

        def score(self, d, rows=slice(None), first=0, size=BLOCK):
            return lax.dot_general(
                qx_ref[self.half, rows], k_ref[self.keys(d, first, size), :],
                (((1,), (1,)), ((), ())), preferred_element_type=jnp.float32)

        def mix(self, d, rows=slice(None), first=0, size=BLOCK, at=0):
            return jnp.dot(weights[rows, at + first:at + first + size],
                           v_ref[self.keys(d, first, size), :], preferred_element_type=jnp.float32)

        def exponents(self, b, at=0, diagonal=False):
            for r in parts:
                for g in groups:
                    if diagonal and r.start < BLOCK and g.start >= PIECE:
                        continue
                    p = jnp.exp2(self.scores[b, r, g] * SCALE - shift[r, :])
                    weights[r, at + g.start:at + g.stop] = p.astype(jnp.bfloat16)

        def tops(self, blocks, diagonal=False):
            for r in parts:
                top = top_ref[r, :]
                query = r.start // BLOCK * PIECE + r.start % PIECE
                query = slice(query, query + PART)
                for b in blocks:
                    for g in groups:
                        if diagonal and r.start < BLOCK and g.start >= PIECE:
                            continue
                        part = self.scores[b, r, g]
                        if diagonal:
                            part = jnp.where(lane[query] + g.start <= row[query], part, FLOOR)
                            self.scores[b, r, g] = part
                        top = jnp.maximum(top, part)
                top_ref[r, :] = top

        def weigh(self, i, blocks):
            for j in range(blocks):
                self.exponents(i + j if late else i + j + 1, j * BLOCK)
            product = self.mix(self.distance(i))
            for j in range(1, blocks):
                product += self.mix(self.distance(i + j), at=j * BLOCK)
            acc[...] += product

        def fresh(self, i, blocks):
            buffers = [i + j if late else i + j + 1 for j in range(blocks)]
            for j in range(blocks):
                self.scores[buffers[j]] = self.score(self.distance(i + j))
            self.tops(buffers)

        def weigh_own(self):
            self.exponents(0, diagonal=True)
            acc[...] = self.mix(0, size=PIECE)
            acc[BLOCK:, :] += self.mix(0, rows=slice(BLOCK, ROWS), first=PIECE, size=PIECE)

        def fresh_own(self):
            self.scores[0, :, 0:PIECE] = self.score(0, size=PIECE)
            self.scores[0, BLOCK:, PIECE:] = self.score(0, slice(BLOCK, ROWS), PIECE, PIECE)
            self.tops([0], diagonal=True)

    def loop(first, stop, old, young):
        def go(i, blocks):
            if old:
                old.weigh(i, blocks)
            if young:
                young.fresh(i, blocks)

        def two(i, carry):
            go(first + 2 * i, 2)
            return carry

        def one(i, carry):
            go(i, 1)
            return carry

        twos = (stop - first) // 2
        lax.fori_loop(0, twos, two, 0)
        lax.fori_loop(first + 2 * twos, stop, one, 0)

    tiles = [Tile(half) for half in range(2)]
    for low, high in ranges:
        lax.fori_loop(jnp.maximum(lowest, low), high, arrive, 0)
    for t in range(3):
        cur = tiles[t - 1] if t > 0 else None
        new = tiles[t] if t < 2 else None
        if cur and not late:
            cur.weigh_own()
        if new and late:
            top_ref[...] = top_in[new.half]
        elif new:
            top_ref[...] = jnp.full((ROWS, D_HEAD), FLOOR, jnp.float32)
            new.fresh_own()
        if cur and new:
            both = jnp.minimum(cur.steps, new.steps)
            loop(0, both, cur, new)
            loop(both, cur.steps, cur, None)
            loop(both, new.steps, None, new)
        elif cur:
            loop(0, cur.steps, cur, None)
        else:
            loop(0, new.steps, None, new)
        if cur and late:
            for rows, tokens, columns in pieces(cur.half):
                mixed = acc[rows, 0:D_HEAD] / acc[rows, D_HEAD:]
                out_ref[tokens, columns] = mixed.astype(jnp.bfloat16)
        elif cur:
            acc_out[cur.half] = acc[...]
        if new:
            for r in parts:
                top = jnp.max(top_ref[r, :], axis=1, keepdims=True)
                top = jnp.broadcast_to(top, (PART, D_HEAD))
                shift[r, :] = top * SCALE
                if late:
                    rescale = jnp.exp2((top_in[new.half, r, :] - top) * SCALE)
                    acc[r, 0:D_HEAD] = acc_in[new.half, r, 0:D_HEAD] * rescale
                    acc[r, D_HEAD:] = acc_in[new.half, r, D_HEAD:] * rescale
                else:
                    top_out[new.half, r, :] = top


def attention(late, doc_starts, q, blocks, state=()):
    vmem = pl.BlockSpec(memory_space=pltpu.VMEM)
    if late:
        out_shape, out_specs = jax.ShapeDtypeStruct(q.shape, jnp.bfloat16), vmem
    else:
        out_shape = (jax.ShapeDtypeStruct((2, ROWS, 2 * D_HEAD), jnp.float32),
                     jax.ShapeDtypeStruct((2, ROWS, D_HEAD), jnp.float32))
        out_specs = (vmem,) * 2
    scores = pltpu.VMEM((6 if late else 4, ROWS, BLOCK), jnp.float32)
    return pl.pallas_call(
        functools.partial(attend, late),
        out_shape=out_shape,
        in_specs=[pl.BlockSpec(memory_space=pltpu.SMEM), vmem]
        + [pl.BlockSpec(memory_space=pl.ANY)] * len(blocks) + [vmem] * len(state),
        out_specs=out_specs,
        scratch_shapes=[
            pltpu.VMEM((SLOTS * BLOCK, 2 * D_HEAD), jnp.bfloat16),
            pltpu.VMEM((SLOTS * BLOCK, 2 * D_HEAD), jnp.bfloat16),
            pltpu.VMEM((2, ROWS, 2 * D_HEAD), jnp.bfloat16),
            scores,
            scores,
            pltpu.VMEM((ROWS, 2 * BLOCK), jnp.bfloat16),
            pltpu.VMEM((ROWS, 2 * D_HEAD), jnp.float32),
            pltpu.VMEM((ROWS, D_HEAD), jnp.float32),
            pltpu.VMEM((ROWS, D_HEAD), jnp.float32),
            pltpu.SemaphoreType.DMA((SLOTS,)),
            pltpu.SemaphoreType.DMA((SLOTS,)),
        ],
        compiler_params=pltpu.CompilerParams(vmem_limit_bytes=(44 if late else 36) * 1024 * 1024),
        cost_estimate=pl.CostEstimate(
            flops=(3 if late else 2) * 10**9, bytes_accessed=4 * 10**6, transcendentals=3 * 10**6
        ),
        name="late_blocks" if late else "early_blocks",
    )(doc_starts, q, *blocks, *state)


def per_device(queries, keys, values, doc_starts):
    devices = lax.axis_size("d")
    rows = queries.shape[0]
    groups = []
    for z in range(0, devices, PLANE):
        groups.append(list(range(z, z + 16)))
        groups.append(list(range(z + 24, z + 32)) + list(range(z + 16, z + 24)))

    def exchange(x):
        return lax.all_to_all(
            x, "d", split_axis=0, concat_axis=0, axis_index_groups=groups, tiled=True
        )

    def move(x, rule):
        pairs = []
        for d in range(devices):
            z, y = d // PLANE, d // ROW % 4
            to = rule(d, z, y)
            if to is not None and to < devices:
                pairs.append((d, to))
        return lax.ppermute(x, "d", pairs)

    def mirror(d, y):
        return d + ROW * (3 - 2 * y)

    def cores(x):
        return move(x, lambda d, z, y: d ^ 1)

    heads = keys.shape[1] // D_HEAD
    kv = jnp.stack(
        [keys.reshape(rows, heads, D_HEAD), values.reshape(rows, heads, D_HEAD)], axis=2
    ).reshape(rows, 2 * heads, D_HEAD).transpose(1, 0, 2)
    own = exchange(kv).reshape(SUPER, D_HEAD)
    q = queries.reshape(rows, 2 * heads, 2 * D_HEAD).transpose(1, 0, 2)
    q = exchange(q).reshape(SUPER, 2 * D_HEAD)

    first_pair = (lax.axis_index("d") & (2 * ROW)) == 0
    z1 = move(own, lambda d, z, y: d + PLANE)
    z2 = move(z1, lambda d, z, y: d + PLANE if z > 0 else None)
    yb = move(z1, lambda d, z, y: mirror(d, y))
    xa = cores(jnp.concatenate([own, z1]))
    z2, q = lax.optimization_barrier((z2, q))
    yac = move(jnp.where(first_pair, own, z2), lambda d, z, y: mirror(d, y))
    xb = cores(jnp.concatenate([z2, yb]))
    state = attention(False, doc_starts, q, (own, z1, xa))
    yac, state = lax.optimization_barrier((yac, state))
    xc = cores(yac)
    out = attention(True, doc_starts, q, (z2, yb, yac, xb, xc), state)
    out = exchange(out.reshape(2 * heads, rows, 2 * D_HEAD))
    return out.transpose(1, 0, 2).reshape(rows, heads * 4 * D_HEAD)


def solution(mesh):
    mesh = Mesh(mesh.devices.reshape(-1), ("d",))
    rows = P("d", None)
    return jax.shard_map(
        per_device, mesh=mesh, in_specs=(rows, rows, rows, P()), out_specs=rows, check_vma=False
    )
```

```python
import functools
import math

import jax
import jax.numpy as jnp
from jax import lax
from jax.experimental import pallas as pl
from jax.experimental.pallas import tpu as pltpu
from jax.sharding import Mesh, PartitionSpec as P

D_HEAD = 128
BLOCK = 512
MAX_DOC = 4096
PLANE = 32
ROW = 8
SUPER = 2 * BLOCK
SLOTS = (MAX_DOC + SUPER) // BLOCK
FLOOR = -1.0e30
SCALE = D_HEAD**-0.5 * math.log2(math.e)
PART = 64
PIECE = BLOCK // 2
ROWS = 2 * BLOCK


def attend(late, starts, q_ref, *refs):
    if late:
        z2, yb, yac, xb, xc, acc_in, top_in, out_ref = refs[:8]
    else:
        own, z1, xa, acc_out, top_out = refs[:5]
    (k_ref, v_ref, qx_ref, scores_a, scores_b, weights, acc, top_ref, shift,
     k_sem, v_sem) = refs[-11:]
    me = lax.axis_index("d")
    z = me // PLANE
    pair = lax.rem(me // (2 * ROW), 2)
    core = lax.rem(me, 2)
    s_first = (z * 2 + pair) * SUPER

    firsts, lasts, counts = [], [], []
    for pos in range(2):
        q_start = s_first + pos * BLOCK
        first = jnp.int32(0)
        last = jnp.int32(0)
        for i in range(starts.shape[0]):
            s = starts[i]
            first = jnp.where(s <= q_start, s, first)
            last = jnp.where(s <= q_start + BLOCK - 1, s, last)
        firsts.append(first)
        lasts.append(last)
        counts.append((q_start - first + BLOCK - 1) // BLOCK)
    lowest = jnp.minimum(SLOTS - 2 - counts[0], SLOTS - 1 - counts[1])

    def fetch(j, mine, mine_row, other, other_row, when):
        swapped = lax.rem(pair + j, 2)
        for half in range(2):
            slot = SLOTS - 2 - 2 * j + lax.bitwise_xor(half, swapped)
            to = pl.ds(pl.multiple_of(slot * BLOCK, BLOCK), BLOCK)
            for c in range(2):
                @pl.when((core == c) & (slot >= lowest) & when)
                def _():
                    mine_at = mine.at[pl.ds(mine_row + half * BLOCK, BLOCK)]
                    other_at = other.at[pl.ds(other_row + half * BLOCK, BLOCK)]
                    k_src, v_src = (mine_at, other_at) if c == 0 else (other_at, mine_at)
                    pltpu.make_async_copy(k_src, k_ref.at[to, 0:D_HEAD], k_sem.at[slot]).start()
                    pltpu.make_async_copy(v_src, v_ref.at[to, 0:D_HEAD], v_sem.at[slot]).start()

    always = me >= 0
    if late:
        fetch(1, yac, 0, xc, 0, pair == 1)
        fetch(1, yb, 0, xb, SUPER, pair == 0)
        fetch(3, yb, 0, xb, SUPER, pair == 1)
        fetch(3, yac, 0, xc, 0, pair == 0)
        fetch(4, z2, 0, xb, 0, always)
        ranges = ((0, 4), (6, 8))
        any_block = z2
    else:
        fetch(0, own, 0, xa, 0, always)
        fetch(2, z1, 0, xa, SUPER, always)
        ranges = ((4, 6), (8, 10))
        any_block = own

    lane = lax.broadcasted_iota(jnp.int32, (BLOCK, D_HEAD), 1)
    row = lax.broadcasted_iota(jnp.int32, (BLOCK, D_HEAD), 0)
    limits = jnp.where(lane == 0, firsts[0], jnp.where(lane == 1, firsts[1],
                       jnp.where(lane == 2, lasts[0], jnp.where(lane == 3, lasts[1], 0))))
    base = s_first - (SLOTS - 2) * BLOCK
    behind = limits - row - base

    def bias(slot, carry):
        to = pl.ds(pl.multiple_of(slot * BLOCK, BLOCK), BLOCK)
        ahead = behind > slot * BLOCK
        k_ref[to, D_HEAD:] = jnp.where(ahead, FLOOR, 0.0).astype(jnp.bfloat16)
        v_ref[to, D_HEAD:] = jnp.ones((BLOCK, D_HEAD), jnp.bfloat16)
        return carry

    def arrive(slot, carry):
        to = pl.ds(pl.multiple_of(slot * BLOCK, BLOCK), BLOCK)
        rows = pl.ds(0, BLOCK)
        pltpu.make_async_copy(any_block.at[rows], k_ref.at[to, 0:D_HEAD], k_sem.at[slot]).wait()
        pltpu.make_async_copy(any_block.at[rows], v_ref.at[to, 0:D_HEAD], v_sem.at[slot]).wait()
        return carry

    for low, high in ranges:
        lax.fori_loop(jnp.maximum(lowest, low), high, bias, 0)

    groups = [slice(g, g + D_HEAD) for g in range(0, BLOCK, D_HEAD)]
    parts = [slice(r, r + PART) for r in range(0, ROWS, PART)]

    def pieces(half):
        for i in range(4):
            part, head = divmod(i, 2)
            first = half * BLOCK + part * PIECE
            yield (slice(i * PIECE, (i + 1) * PIECE), slice(first, first + PIECE),
                   slice(head * D_HEAD, (head + 1) * D_HEAD))

    class Tile:
        def __init__(self, half):
            self.half = half
            self.scores = scores_b if half else scores_a
            pos = lax.bitwise_xor(half, pair)
            self.own = SLOTS - 2 + pos
            n = jnp.where(pos == 0, counts[0], counts[1])
            border = jnp.where(pos == 0, lasts[0], lasts[1]) - s_first - pos * BLOCK
            column = jnp.where(row >= border, pos + 2, pos)
            marks = jnp.where((lane == pos) | (lane == column), 1.0, 0.0).astype(jnp.bfloat16)
            for rows, tokens, columns in pieces(half):
                qx_ref[half, rows, 0:D_HEAD] = q_ref[tokens, columns]
                query = tokens.start % BLOCK
                qx_ref[half, rows, D_HEAD:] = marks[query:query + PIECE]
            m = n - pos
            if late:
                self.steps = jnp.clip(m, 0, 2) + jnp.clip(m - 4, 0, 4)
                self.distance = lambda i: jnp.where(i < 2, i + 1, i + 3) + pos
            else:
                beside = jnp.where((pos == 1) & (n >= 1), 1, 0)
                self.steps = beside + jnp.clip(m - 2, 0, 2)
                self.distance = lambda i: jnp.where((pos == 1) & (i == 0), 1, i + 3)

        def keys(self, d, first=0, size=BLOCK):
            return pl.ds(pl.multiple_of((self.own - d) * BLOCK + first, PIECE), size)

        def score(self, d, rows=slice(None), first=0, size=BLOCK):
            return lax.dot_general(
                qx_ref[self.half, rows], k_ref[self.keys(d, first, size), :],
                (((1,), (1,)), ((), ())), preferred_element_type=jnp.float32)

        def mix(self, d, rows=slice(None), first=0, size=BLOCK, at=0):
            return jnp.dot(weights[rows, at + first:at + first + size],
                           v_ref[self.keys(d, first, size), :], preferred_element_type=jnp.float32)

        def exponents(self, b, at=0, diagonal=False):
            for r in parts:
                for g in groups:
                    if diagonal and r.start < BLOCK and g.start >= PIECE:
                        continue
                    p = jnp.exp2(self.scores[b, r, g] * SCALE - shift[r, :])
                    weights[r, at + g.start:at + g.stop] = p.astype(jnp.bfloat16)

        def tops(self, blocks, diagonal=False):
            for r in parts:
                top = top_ref[r, :]
                query = r.start // BLOCK * PIECE + r.start % PIECE
                query = slice(query, query + PART)
                for b in blocks:
                    for g in groups:
                        if diagonal and r.start < BLOCK and g.start >= PIECE:
                            continue
                        part = self.scores[b, r, g]
                        if diagonal:
                            part = jnp.where(lane[query] + g.start <= row[query], part, FLOOR)
                            self.scores[b, r, g] = part
                        top = jnp.maximum(top, part)
                top_ref[r, :] = top

        def weigh(self, i, blocks):
            for j in range(blocks):
                self.exponents(i + j if late else i + j + 1, j * BLOCK)
            product = self.mix(self.distance(i))
            for j in range(1, blocks):
                product += self.mix(self.distance(i + j), at=j * BLOCK)
            acc[...] += product

        def fresh(self, i, blocks):
            buffers = [i + j if late else i + j + 1 for j in range(blocks)]
            for j in range(blocks):
                self.scores[buffers[j]] = self.score(self.distance(i + j))
            self.tops(buffers)

        def weigh_own(self):
            self.exponents(0, diagonal=True)
            acc[...] = self.mix(0, size=PIECE)
            acc[BLOCK:, :] += self.mix(0, rows=slice(BLOCK, ROWS), first=PIECE, size=PIECE)

        def fresh_own(self):
            self.scores[0, :, 0:PIECE] = self.score(0, size=PIECE)
            self.scores[0, BLOCK:, PIECE:] = self.score(0, slice(BLOCK, ROWS), PIECE, PIECE)
            self.tops([0], diagonal=True)

    def loop(first, stop, old, young):
        def go(i, blocks):
            if old:
                old.weigh(i, blocks)
            if young:
                young.fresh(i, blocks)

        def two(i, carry):
            go(first + 2 * i, 2)
            return carry

        def one(i, carry):
            go(i, 1)
            return carry

        twos = (stop - first) // 2
        lax.fori_loop(0, twos, two, 0)
        lax.fori_loop(first + 2 * twos, stop, one, 0)

    tiles = [Tile(half) for half in range(2)]
    for low, high in ranges:
        lax.fori_loop(jnp.maximum(lowest, low), high, arrive, 0)
    for t in range(3):
        cur = tiles[t - 1] if t > 0 else None
        new = tiles[t] if t < 2 else None
        if cur and not late:
            cur.weigh_own()
        if new and late:
            top_ref[...] = top_in[new.half]
        elif new:
            top_ref[...] = jnp.full((ROWS, D_HEAD), FLOOR, jnp.float32)
            new.fresh_own()
        if cur and new:
            both = jnp.minimum(cur.steps, new.steps)
            loop(0, both, cur, new)
            loop(both, cur.steps, cur, None)
            loop(both, new.steps, None, new)
        elif cur:
            loop(0, cur.steps, cur, None)
        else:
            loop(0, new.steps, None, new)
        if cur and late:
            for rows, tokens, columns in pieces(cur.half):
                mixed = acc[rows, 0:D_HEAD] / acc[rows, D_HEAD:]
                out_ref[tokens, columns] = mixed.astype(jnp.bfloat16)
        elif cur:
            acc_out[cur.half] = acc[...]
        if new:
            for r in parts:
                top = jnp.max(top_ref[r, :], axis=1, keepdims=True)
                top = jnp.broadcast_to(top, (PART, D_HEAD))
                shift[r, :] = top * SCALE
                if late:
                    rescale = jnp.exp2((top_in[new.half, r, :] - top) * SCALE)
                    acc[r, 0:D_HEAD] = acc_in[new.half, r, 0:D_HEAD] * rescale
                    acc[r, D_HEAD:] = acc_in[new.half, r, D_HEAD:] * rescale
                else:
                    top_out[new.half, r, :] = top


def attention(late, doc_starts, q, blocks, state=()):
    vmem = pl.BlockSpec(memory_space=pltpu.VMEM)
    if late:
        out_shape, out_specs = jax.ShapeDtypeStruct(q.shape, jnp.bfloat16), vmem
    else:
        out_shape = (jax.ShapeDtypeStruct((2, ROWS, 2 * D_HEAD), jnp.float32),
                     jax.ShapeDtypeStruct((2, ROWS, D_HEAD), jnp.float32))
        out_specs = (vmem,) * 2
    scores = pltpu.VMEM((6 if late else 4, ROWS, BLOCK), jnp.float32)
    return pl.pallas_call(
        functools.partial(attend, late),
        out_shape=out_shape,
        in_specs=[pl.BlockSpec(memory_space=pltpu.SMEM), vmem]
        + [pl.BlockSpec(memory_space=pl.ANY)] * len(blocks) + [vmem] * len(state),
        out_specs=out_specs,
        scratch_shapes=[
            pltpu.VMEM((SLOTS * BLOCK, 2 * D_HEAD), jnp.bfloat16),
            pltpu.VMEM((SLOTS * BLOCK, 2 * D_HEAD), jnp.bfloat16),
            pltpu.VMEM((2, ROWS, 2 * D_HEAD), jnp.bfloat16),
            scores,
            scores,
            pltpu.VMEM((ROWS, 2 * BLOCK), jnp.bfloat16),
            pltpu.VMEM((ROWS, 2 * D_HEAD), jnp.float32),
            pltpu.VMEM((ROWS, D_HEAD), jnp.float32),
            pltpu.VMEM((ROWS, D_HEAD), jnp.float32),
            pltpu.SemaphoreType.DMA((SLOTS,)),
            pltpu.SemaphoreType.DMA((SLOTS,)),
        ],
        compiler_params=pltpu.CompilerParams(vmem_limit_bytes=(44 if late else 36) * 1024 * 1024),
        cost_estimate=pl.CostEstimate(
            flops=(3 if late else 2) * 10**9, bytes_accessed=4 * 10**6, transcendentals=3 * 10**6
        ),
        name="late_blocks" if late else "early_blocks",
    )(doc_starts, q, *blocks, *state)


def per_device(queries, keys, values, doc_starts):
    devices = lax.axis_size("d")
    rows = queries.shape[0]
    groups = []
    for z in range(0, devices, PLANE):
        groups.append(list(range(z, z + 16)))
        groups.append(list(range(z + 24, z + 32)) + list(range(z + 16, z + 24)))

    def exchange(x):
        return lax.all_to_all(
            x, "d", split_axis=0, concat_axis=0, axis_index_groups=groups, tiled=True
        )

    def move(x, rule):
        pairs = []
        for d in range(devices):
            z, y = d // PLANE, d // ROW % 4
            to = rule(d, z, y)
            if to is not None and to < devices:
                pairs.append((d, to))
        return lax.ppermute(x, "d", pairs)

    def mirror(d, y):
        return d + ROW * (3 - 2 * y)

    def cores(x):
        return move(x, lambda d, z, y: d ^ 1)

    heads = keys.shape[1] // D_HEAD
    kv = jnp.stack(
        [keys.reshape(rows, heads, D_HEAD), values.reshape(rows, heads, D_HEAD)], axis=2
    ).reshape(rows, 2 * heads, D_HEAD).transpose(1, 0, 2)
    own = exchange(kv).reshape(SUPER, D_HEAD)
    q = queries.reshape(rows, 2 * heads, 2 * D_HEAD).transpose(1, 0, 2)
    q = exchange(q).reshape(SUPER, 2 * D_HEAD)

    first_pair = (lax.axis_index("d") & (2 * ROW)) == 0
    z1 = move(own, lambda d, z, y: d + PLANE)
    z2 = move(z1, lambda d, z, y: d + PLANE if z > 0 else None)
    yb = move(z1, lambda d, z, y: mirror(d, y))
    xa = cores(jnp.concatenate([own, z1]))
    z2, q = lax.optimization_barrier((z2, q))
    yac = move(jnp.where(first_pair, own, z2), lambda d, z, y: mirror(d, y))
    xb = cores(jnp.concatenate([z2, yb]))
    state = attention(False, doc_starts, q, (own, z1, xa))
    yac, state = lax.optimization_barrier((yac, state))
    xc = cores(yac)
    out = attention(True, doc_starts, q, (z2, yb, yac, xb, xc), state)
    out = exchange(out.reshape(2 * heads, rows, 2 * D_HEAD))
    return out.transpose(1, 0, 2).reshape(rows, heads * 4 * D_HEAD)


def solution(mesh):
    mesh = Mesh(mesh.devices.reshape(-1), ("d",))
    rows = P("d", None)
    return jax.shard_map(
        per_device, mesh=mesh, in_specs=(rows, rows, rows, P()), out_specs=rows, check_vma=False
    )
```
